32 devices in a mesh: tm: 4 (over y, core), space: 8 (over z, x).
Axes of the slice: x: 2, y: 2, z: 4, core: 2. Of those that a mesh axis runs over, the one named last changes fastest.
Arguments:
- init_states: float32 [2, 4, 256, 16, 128], P(None, 'tm', None, 'space'), may hold values from -6 to 6
- forcing: float32 [2, 256, 16, 128], P(None, None, 'space'), may hold values from -6 to 6
- damp: float32 [2, 256, 16, 128], P(None, None, 'space'), may hold values from 0.3 to 0.95
- kappa_x: float32 [256], replicated, may hold values from 2 to 60
- kappa_y: float32 [16], replicated, may hold values from 2 to 60
- kappa_z: float32 [128], replicated, may hold values from 0.02 to 0.24
- sea_tiles: int32 [16, 1], replicated, may hold values 0 or 1
- phases: int32 [4], P('tm'), may hold values from 0 to 11
Outputs:
- slab_starts: float32 [2, 4, 256, 16, 128], P(None, 'tm', None, 'space')
The draws below stay inside these ranges and needn't reach their ends.
All inputs are finite; a program needn't handle non-finite values.
Results may differ from the reference program's by a relative error of at most 0.0003.
Values sent between devices are 32-bit elements; how exact they have to be, the bound alone decides.
A program may use at most 64 MiB of HBM per device.

```python
import math
import jax
import jax.numpy as jnp
from jax import lax

NX = 256
NY = 16
NZ = 128
TRACERS = 2
SLABS = 4
STEPS = 2
ITERS = 2
TILE = 16
PHASES = 12


def place_ends(values, key, smallest, largest):
    spot = [jax.random.randint(jax.random.fold_in(key, axis), (), 0, length) for axis, length in enumerate(values.shape)]
    longest = values.shape.index(max(values.shape))
    next_to = spot[:longest] + [(spot[longest] + 1) % values.shape[longest]] + spot[longest + 1:]
    return values.at[tuple(spot)].set(smallest).at[tuple(next_to)].set(largest)


def block_scale(stream_key, dims, split, low, high):
    level, own = 1.0, jax.random.fold_in(stream_key, 6)
    for axis_at, parts in split:
        draws = jnp.exp(jax.random.uniform(jax.random.fold_in(own, axis_at), (parts,), jnp.float32, low / len(split), high / len(split)))
        level = level * jnp.repeat(draws, dims[axis_at] // parts).reshape([-1 if axis == axis_at else 1 for axis in range(len(dims))])
    return level


def normal_values(key, dims, spread, reach, split=(), kind=jnp.bfloat16):
    loudness = block_scale(key, dims, split, -0.22, 0.18) if split else 1.0
    array = jax.random.normal(key, dims, jnp.float32) * spread * loudness
    return jnp.minimum(jnp.maximum(array, -reach), reach).astype(kind)


def setup_inputs(seed: int = 0) -> dict:
    seeds = jax.random.split(jax.random.key(seed), 9)
    init_states = normal_values(seeds[0], (TRACERS, SLABS, NX, NY, NZ), 1.0, 6.0, ((1, 4), (3, 8)), jnp.float32)
    forcing = normal_values(seeds[1], (TRACERS, NX, NY, NZ), 1.0, 6.0, ((2, 8),), jnp.float32)
    damp = jnp.clip(jnp.exp(math.log(0.95) - 1.1526795 * jax.random.uniform(seeds[2], (TRACERS, NX, NY, NZ), jnp.float32) ** block_scale(seeds[2], (TRACERS, NX, NY, NZ), ((2, 8),), -0.2, 0.2)), 0.3, 0.95)
    kappa_x = jnp.clip(jnp.exp(jax.random.uniform(seeds[3], (NX,), jnp.float32, math.log(2.0), math.log(60.0))), 2.0, 60.0)
    kappa_y = jnp.clip(jnp.exp(jax.random.uniform(seeds[4], (NY,), jnp.float32, math.log(2.0), math.log(60.0))), 2.0, 60.0)
    kappa_z = jnp.clip(jax.random.uniform(seeds[5], (NZ,), jnp.float32, 0.02, 0.24), 0.02, 0.24)
    sea_tiles = place_ends((jax.random.randint(seeds[6], (NX // TILE, NY // TILE), 0, 4) < 3).astype(jnp.int32), jax.random.fold_in(seeds[6], 1), 0, 1)
    phases = place_ends(jax.random.randint(seeds[7], (SLABS,), 0, PHASES), jax.random.fold_in(seeds[7], 1), 0, PHASES - 1).astype(jnp.int32)
    return dict(init_states=init_states, forcing=forcing, damp=damp, kappa_x=kappa_x, kappa_y=kappa_y, kappa_z=kappa_z, sea_tiles=sea_tiles, phases=phases)


def line_coefficients(kappa):
    face = 0.5 * (kappa[1:] + kappa[:-1])
    zero = jnp.zeros((1,), kappa.dtype)
    left = jnp.concatenate([zero, face])
    right = jnp.concatenate([face, zero])
    return (-left, 1.0 + left + right, -right)

def solve_lines(field, kappa):
    lower, middle, upper = line_coefficients(kappa)
    batch = field.shape[:-1]
    return lax.linalg.tridiagonal_solve(jnp.broadcast_to(lower, batch), jnp.broadcast_to(middle, batch), jnp.broadcast_to(upper, batch), field)

def solve_x(field, kappa_x):
    shape = field.shape
    flat = field.reshape(shape[0], shape[1], shape[2] * shape[3])
    return solve_lines(flat, kappa_x).reshape(shape)

def vertical_mix(field, kappa_z):
    face = 0.5 * (kappa_z[1:] + kappa_z[:-1])
    flux = face * (field[..., 1:] - field[..., :-1])
    zeros = jnp.zeros(field.shape[:-1] + (1,), field.dtype)
    flux = jnp.concatenate([zeros, flux, zeros], axis=-1)
    return field + flux[..., 1:] - flux[..., :-1]

def fine_map(field, phase, source, kappa_x, kappa_y, kappa_z):
    for step in range(STEPS):
        if step % 2 == 0:
            field = solve_lines(solve_x(field, kappa_x), kappa_y)
        else:
            field = solve_x(solve_lines(field, kappa_y), kappa_x)
        amplitude = jnp.cos(2.0 * math.pi * (phase * STEPS + step) / (PHASES * STEPS))
        field = vertical_mix(field, kappa_z) + amplitude * source
    return field

def reference(init_states, forcing, damp, kappa_x, kappa_y, kappa_z, sea_tiles, phases):
    tiles = sea_tiles.astype(jnp.float32)
    sea = jnp.repeat(jnp.repeat(tiles, TILE, axis=0), TILE, axis=1)
    source = forcing * sea[None, :, :, None]
    phase_float = phases.astype(jnp.float32)
    log_damp = jnp.log(damp)
    states = init_states
    for iteration in range(ITERS):
        starts = jnp.moveaxis(states, 1, 0)
        ends = lax.map(lambda item: fine_map(item[0], item[1], source, kappa_x, kappa_y, kappa_z), (starts, phase_float.reshape(SLABS, 1, 1, 1, 1)))
        factors = []
        offsets = []
        for slab in range(SLABS):
            weight = 1.0 + 0.5 * jnp.cos(2.0 * math.pi * phase_float[slab] / PHASES)
            factor = jnp.exp(weight * log_damp)
            factors.append(factor)
            offsets.append(ends[slab] - factor * starts[slab])
        product = jnp.ones_like(damp)
        total = jnp.zeros_like(damp)
        for slab in range(SLABS):
            product = factors[slab] * product
            total = factors[slab] * total + offsets[slab]
        first = total / (1.0 - product)
        fresh = [first]
        for slab in range(SLABS - 1):
            fresh.append(factors[slab] * fresh[-1] + offsets[slab])
        states = jnp.stack(fresh, axis=1)
    return states
```

```python
import functools
import math

import jax
import jax.numpy as jnp
from jax import lax
from jax.experimental import pallas as pl
from jax.experimental.pallas import tpu as pltpu
from jax.sharding import PartitionSpec as P

STEPS = 2
ITERS = 2
TILE = 16
PHASES = 12


def shifted(array, axis, by):
    devices = lax.axis_size(axis)
    return lax.ppermute(array, axis, [(i, (i + by) % devices) for i in range(devices)])


def line_inverse(kappa):
    face = 0.5 * (kappa[1:] + kappa[:-1])
    zero = jnp.zeros((1,), kappa.dtype)
    left = jnp.concatenate([zero, face])
    right = jnp.concatenate([face, zero])
    identity = jnp.eye(kappa.shape[0], dtype=kappa.dtype)
    return lax.linalg.tridiagonal_solve(-left, 1.0 + left + right, -right, identity)


def solve_lines(field, inverse):
    return jnp.matmul(inverse, field, precision=lax.Precision.HIGHEST)


def solve_x(field, inverse):
    shape = field.shape
    flat = field.reshape(shape[0], shape[1], shape[2], shape[3] * shape[4])
    return solve_lines(flat, inverse).reshape(shape)


def vertical_mix(field, kappa_z):
    face = 0.5 * (kappa_z[1:] + kappa_z[:-1])
    flux = face * (field[..., 1:] - field[..., :-1])
    zeros = jnp.zeros(field.shape[:-1] + (1,), field.dtype)
    flux = jnp.concatenate([zeros, flux, zeros], axis=-1)
    return field + flux[..., 1:] - flux[..., :-1]


def compose(earlier, later):
    return (earlier[0] * later[0], later[0] * earlier[1] + later[1])


def column_pass(field, inverse_y):
    return lax.all_to_all(
        solve_lines(
            lax.all_to_all(field, "space", split_axis=2, concat_axis=3, tiled=True), inverse_y
        ),
        "space",
        split_axis=3,
        concat_axis=2,
        tiled=True,
    )


def body(init_states, forcing, damp, kappa_x, kappa_y, kappa_z, sea_tiles, phases):
    row_count = init_states.shape[3]
    inverse_x = line_inverse(kappa_x)
    inverse_y = line_inverse(kappa_y)
    tiles = sea_tiles.astype(jnp.float32)
    sea = jnp.repeat(jnp.repeat(tiles, TILE, axis=0), TILE, axis=1)
    sea_rows = lax.dynamic_slice_in_dim(sea, lax.axis_index("space") * row_count, row_count, 1)
    source = (forcing * sea_rows[None, :, :, None])[:, None]
    phase_float = phases.astype(jnp.float32)
    weight = 1.0 + 0.5 * jnp.cos(2.0 * math.pi * phase_float / PHASES)
    factors = jnp.exp(weight[None, :, None, None, None] * jnp.log(damp)[:, None])
    states = init_states
    for iteration in range(ITERS):
        field = states
        for step in range(STEPS):
            amplitude = jnp.cos(2.0 * math.pi * (phase_float * STEPS + step) / (PHASES * STEPS))[
                None, :, None, None, None
            ]
            if step % 2 == 0:
                field = column_pass(solve_x(field, inverse_x), inverse_y)
            else:
                field = solve_x(column_pass(field, inverse_y), inverse_x)
            field = vertical_mix(field, kappa_z) + amplitude * source
        offsets = field - factors * states
        own_factor = factors[:, 0]
        own_offset = offsets[:, 0]
        own = (own_factor, own_offset)
        ident = (jnp.ones_like(own_factor), jnp.zeros_like(own_offset))
        count = lax.axis_size("tm")
        here = lax.axis_index("tm")
        lower_part = ident
        upper_part = ident
        moving = jnp.stack([own_factor, own_offset])
        for turn in range(1, count):
            moving = shifted(moving, "tm", 1)
            piece = (moving[0], moving[1])
            anchor = (here - turn) % count
            before = anchor < here
            joined_low = compose(piece, lower_part)
            joined_high = compose(piece, upper_part)
            lower_part = (
                jnp.where(before, joined_low[0], lower_part[0]),
                jnp.where(before, joined_low[1], lower_part[1]),
            )
            upper_part = (
                jnp.where(before, upper_part[0], joined_high[0]),
                jnp.where(before, upper_part[1], joined_high[1]),
            )
        period = compose(compose(lower_part, own), upper_part)
        first = period[1] / (1.0 - period[0])
        start = lower_part[0] * first + lower_part[1]
        fresh = [start]
        states = jnp.stack(fresh, axis=1)
    return states


LANES = 128
HALO = 2 * ITERS
MESH = pl.DeviceIdType.MESH


def dot(a, b):
    return jnp.dot(a, b, precision=lax.Precision.HIGHEST, preferred_element_type=jnp.float32)


def iota(shape, axis):
    return lax.broadcasted_iota(jnp.int32, shape, axis)


def faces(kappa_row, n):
    row, col = iota((n, n), 0), iota((n, n), 1)
    own = jnp.sum(jnp.where(row == col, kappa_row, 0.0), axis=1, keepdims=True)
    face = 0.5 * (own + kappa_row)
    below = jnp.where(col == row - 1, face, 0.0)
    above = jnp.where(col == row + 1, face, 0.0)
    return (
        jnp.sum(below, axis=1, keepdims=True),
        jnp.sum(above, axis=1, keepdims=True),
        below + above,
    )


def reduced_inverse(kappa_row, n):
    lower, upper, _ = faces(kappa_row, n)
    shape = (n, LANES)
    a = jnp.broadcast_to(-lower, shape)
    c = jnp.broadcast_to(-upper, shape)
    b = 1.0 - a - c
    blocks = [
        (iota(shape, 0) == iota(shape, 1) + LANES * j).astype(jnp.float32)
        for j in range(max(n // LANES, 1))
    ]
    s = 1
    while s < n:
        before = functools.partial(pltpu.roll, shift=s, axis=0)
        after = functools.partial(pltpu.roll, shift=n - s, axis=0)
        alpha = -a / before(b)
        gamma = -c / after(b)
        blocks = [d + alpha * before(d) + gamma * after(d) for d in blocks]
        b = b + alpha * before(c) + gamma * after(a)
        a, c = alpha * before(a), gamma * after(c)
        s *= 2
    inverse = 1.0 / b
    return [d * inverse for d in blocks]


def period_kernel(
    size, u_ref, f_ref, damp_ref, kx_ref, ky_ref, kz_ref, sea_ref, phase_ref, out_ref,
    ubuf, fbuf, pbuf, xbuf, dbuf, qbuf, obuf, rbuf, g_ref, a_ref, state, factor, source, offset_ref,
    u_send, u_recv, f_send, f_recv, p_send, p_recv, o_send, o_recv,
):
    n_tm, n_sp, n_t, nx, rows, nz = size
    count = n_tm * n_sp
    per = count // n_t
    chunk = nz // per
    window = chunk + 2 * HALO
    halves = nx // LANES
    wrows = window * rows
    crows = chunk * rows
    all_rows = n_sp * wrows
    ny = n_sp * rows

    here = lax.axis_index("tm")
    spot = lax.axis_index("space")
    me = here * n_sp + spot

    def window_start(k):
        return jnp.minimum(jnp.maximum(k * chunk - HALO, 0), nz - window)

    def window_rows(k):
        return pl.ds(pl.multiple_of(window_start(k) * rows, 8), wrows)

    def chunk_rows(k):
        return pl.ds(pl.multiple_of(k * crows, 8), crows)

    def device(index):
        return {"tm": index // n_sp, "space": index % n_sp}

    barrier = pltpu.get_barrier_semaphore()

    @pl.loop(1, count)
    def greet(offset):
        pl.semaphore_signal(
            barrier, inc=1, device_id=device((me + offset) % count), device_id_type=MESH
        )

    def turn(ref, buf, where):
        for t in range(n_t):
            for half in range(halves):
                for y in range(rows):
                    part = ref[t, pl.ds(half * LANES * rows + y, LANES, stride=rows), :]
                    buf[(t, *where, half, pl.ds(y, nz, stride=rows), slice(None))] = part.T

    turn(u_ref, ubuf, ())
    turn(damp_ref, fbuf, (0,))
    turn(f_ref, fbuf, (1,))
    pbuf[...] = jnp.full((8, LANES), phase_ref[0].astype(jnp.float32))

    my_t, my_k = me // per, me % per
    my_start = window_start(my_k)

    own_copies = [
        pltpu.make_async_copy(
            ubuf.at[my_t, :, window_rows(my_k), :], xbuf.at[here, spot], u_recv.at[me]
        ),
        pltpu.make_async_copy(
            fbuf.at[my_t, :, :, window_rows(my_k), :], dbuf.at[spot], f_recv.at[spot]
        ),
        pltpu.make_async_copy(pbuf, qbuf.at[here], p_recv.at[here]),
    ]

    def send_u(offset):
        index = (me + offset) % count
        return pltpu.make_async_remote_copy(
            src_ref=ubuf.at[index // per, :, window_rows(index % per), :],
            dst_ref=xbuf.at[here, spot],
            send_sem=u_send.at[offset],
            recv_sem=u_recv.at[me],
            device_id=device(index),
            device_id_type=MESH,
        )

    def send_f(offset):
        index = here * n_sp + (spot + offset) % n_sp
        return pltpu.make_async_remote_copy(
            src_ref=fbuf.at[index // per, :, :, window_rows(index % per), :],
            dst_ref=dbuf.at[spot],
            send_sem=f_send.at[offset],
            recv_sem=f_recv.at[spot],
            device_id=device(index),
            device_id_type=MESH,
        )

    def send_p(offset):
        return pltpu.make_async_remote_copy(
            src_ref=pbuf,
            dst_ref=qbuf.at[here],
            send_sem=p_send.at[offset],
            recv_sem=p_recv.at[here],
            device_id={"tm": (here + offset) % n_tm, "space": spot},
            device_id_type=MESH,
        )

    def send_o(offset):
        index = (me + offset) % count
        inner = pl.multiple_of((my_k * chunk - my_start) * rows, 8)
        return pltpu.make_async_remote_copy(
            src_ref=obuf.at[index // n_sp, index % n_sp, :, pl.ds(inner, crows), :],
            dst_ref=rbuf.at[my_t, :, chunk_rows(my_k), :],
            send_sem=o_send.at[offset],
            recv_sem=o_recv.at[me],
            device_id=device(index),
            device_id_type=MESH,
        )

    pl.semaphore_wait(barrier, count - 1)

    @pl.loop(1, n_tm)
    def start_p(offset):
        send_p(offset).start()

    @pl.loop(1, count)
    def start_u(offset):
        send_u(offset).start()

    @pl.loop(1, n_sp)
    def start_f(offset):
        send_f(offset).start()

    for copy in own_copies:
        copy.start()

    for half, block in enumerate(reduced_inverse(kx_ref[...], nx)):
        a_ref[0, :, half * LANES : (half + 1) * LANES] = block
    a_ref[1] = dot(a_ref[0], a_ref[0])
    q, j = iota((all_rows, ny), 0), iota((all_rows, ny), 1)
    line = (q // wrows) * rows + q % rows
    pick_y = (line == j).astype(jnp.float32)
    q, j = iota((LANES, all_rows), 1), iota((LANES, all_rows), 0)
    line = (q // wrows) * rows + q % rows
    pick_y_back = (line == j).astype(jnp.float32)
    big_y = dot(dot(pick_y, reduced_inverse(ky_ref[...], ny)[0]), pick_y_back)
    _, _, beside = faces(kz_ref[...], nz)
    identity = (iota((nz, nz), 0) == iota((nz, nz), 1)).astype(jnp.float32)
    vertical = beside + identity * (1.0 - jnp.sum(beside, axis=1, keepdims=True))
    q, j = iota((all_rows, nz), 0), iota((all_rows, nz), 1)
    pick_z = (my_start + (q % wrows) // rows == j).astype(jnp.float32)
    q, j = iota((nz, all_rows), 1), iota((nz, all_rows), 0)
    pick_z_back = (my_start + (q % wrows) // rows == j).astype(jnp.float32)
    g_ref[0] = big_y * dot(dot(pick_z, vertical), pick_z_back)
    g_ref[1] = dot(g_ref[0], g_ref[0])
    tile = (iota((nx // TILE, nx), 1) // TILE == iota((nx // TILE, nx), 0)).astype(jnp.float32)
    sea = jnp.sum(sea_ref[...].astype(jnp.float32) * tile, axis=0, keepdims=True)

    def gathered(ref, where):
        return jnp.concatenate(
            [ref[where(half)].reshape(all_rows, LANES) for half in range(halves)], axis=1
        )

    own_copies[1].wait()
    own_copies[2].wait()

    @pl.loop(1, n_tm)
    def wait_p(offset):
        index = (here + n_tm - offset) % n_tm
        pltpu.make_async_copy(qbuf.at[index], qbuf.at[index], p_recv.at[index]).wait()

    @pl.loop(1, n_sp)
    def wait_f(offset):
        index = (spot + n_sp - offset) % n_sp
        pltpu.make_async_copy(dbuf.at[index], dbuf.at[index], f_recv.at[index]).wait()

    source[1] = gathered(dbuf, lambda half: (slice(None), 1, half)) * sea
    source[0] = dot(dot(g_ref[0], source[1]), a_ref[0])

    @pl.loop(0, n_tm)
    def make_factors(n):
        log_damp = jnp.log(gathered(dbuf, lambda half: (slice(None), 0, half)))
        phase = qbuf[n]
        weight = 1.0 + 0.5 * jnp.cos(2.0 * math.pi * phase / PHASES)
        first = jnp.cos(2.0 * math.pi * (phase * STEPS) / (PHASES * STEPS))
        second = jnp.cos(2.0 * math.pi * (phase * STEPS + 1) / (PHASES * STEPS))

        def wide(values):
            return jnp.concatenate([values[:1]] * halves, axis=1)

        factor[n] = jnp.exp(wide(weight) * log_damp)
        offset_ref[n] = wide(first) * source[0] + wide(second) * source[1]

    own_copies[0].wait()

    @pl.loop(1, count)
    def wait_u(offset):
        index = (me + count - offset) % count
        slot = xbuf.at[index // n_sp, index % n_sp]
        pltpu.make_async_copy(slot, slot, u_recv.at[index]).wait()

    @pl.loop(0, n_tm)
    def take(n):
        state[n] = gathered(xbuf, lambda half: (n, slice(None), half))

    for iteration in range(ITERS):

        @pl.loop(0, n_tm)
        def fine(n):
            field = state[n]
            moved = dot(dot(g_ref[1], field), a_ref[1])
            state[n] = moved + offset_ref[n] - factor[n] * field

        product = factor[0]
        total = state[0]
        for n in range(1, n_tm):
            product = factor[n] * product
            total = factor[n] * total + state[n]
        fresh = total / (1.0 - product)
        for n in range(n_tm):
            later = factor[n] * fresh + state[n]
            state[n] = fresh
            fresh = later

    @pl.loop(0, n_tm)
    def put(n):
        for half in range(halves):
            obuf[n, :, half] = state[n, :, half * LANES : (half + 1) * LANES].reshape(
                n_sp, wrows, LANES
            )

    inner = pl.multiple_of((my_k * chunk - my_start) * rows, 8)
    back = pltpu.make_async_copy(
        obuf.at[here, spot, :, pl.ds(inner, crows), :],
        rbuf.at[my_t, :, chunk_rows(my_k), :],
        o_recv.at[me],
    )

    @pl.loop(1, count)
    def start_o(offset):
        send_o(offset).start()

    back.start()
    back.wait()

    @pl.loop(1, count)
    def wait_o(offset):
        index = (me + count - offset) % count
        slot = rbuf.at[index // per, :, chunk_rows(index % per), :]
        pltpu.make_async_copy(slot, slot, o_recv.at[index]).wait()

    for t in range(n_t):
        for half in range(halves):
            for y in range(rows):
                part = rbuf[t, half, pl.ds(y, nz, stride=rows), :]
                out_ref[t, pl.ds(half * LANES * rows + y, LANES, stride=rows), :] = part.T

    @pl.loop(1, count)
    def sent(offset):
        send_u(offset).wait_send()
        send_o(offset).wait_send()

    @pl.loop(1, n_sp)
    def sent_f(offset):
        send_f(offset).wait_send()

    @pl.loop(1, n_tm)
    def sent_p(offset):
        send_p(offset).wait_send()


def whole_period(init_states, forcing, damp, kappa_x, kappa_y, kappa_z, sea_tiles, phases):
    n_tm, n_sp = lax.axis_size("tm"), lax.axis_size("space")
    n_t, _, nx, rows, nz = init_states.shape
    count = n_tm * n_sp
    chunk = nz // (count // n_t)
    window = chunk + 2 * HALO
    halves = nx // LANES
    wrows = window * rows
    all_rows = n_sp * wrows
    flat = (n_t, nx * rows, nz)
    vmem = pl.BlockSpec(memory_space=pltpu.VMEM)
    f32 = jnp.float32
    out = pl.pallas_call(
        functools.partial(period_kernel, (n_tm, n_sp, n_t, nx, rows, nz)),
        out_shape=jax.ShapeDtypeStruct(flat, f32),
        in_specs=[vmem] * 7 + [pl.BlockSpec(memory_space=pltpu.SMEM)],
        out_specs=vmem,
        scratch_shapes=[
            pltpu.VMEM((n_t, halves, nz * rows, LANES), f32),
            pltpu.VMEM((n_t, 2, halves, nz * rows, LANES), f32),
            pltpu.VMEM((8, LANES), f32),
            pltpu.VMEM((n_tm, n_sp, halves, wrows, LANES), f32),
            pltpu.VMEM((n_sp, 2, halves, wrows, LANES), f32),
            pltpu.VMEM((n_tm, 8, LANES), f32),
            pltpu.VMEM((n_tm, n_sp, halves, wrows, LANES), f32),
            pltpu.VMEM((n_t, halves, nz * rows, LANES), f32),
            pltpu.VMEM((2, all_rows, all_rows), f32),
            pltpu.VMEM((2, nx, nx), f32),
            pltpu.VMEM((n_tm, all_rows, nx), f32),
            pltpu.VMEM((n_tm, all_rows, nx), f32),
            pltpu.VMEM((2, all_rows, nx), f32),
            pltpu.VMEM((n_tm, all_rows, nx), f32),
            pltpu.SemaphoreType.DMA((count,)),
            pltpu.SemaphoreType.DMA((count,)),
            pltpu.SemaphoreType.DMA((n_sp,)),
            pltpu.SemaphoreType.DMA((n_sp,)),
            pltpu.SemaphoreType.DMA((n_tm,)),
            pltpu.SemaphoreType.DMA((n_tm,)),
            pltpu.SemaphoreType.DMA((count,)),
            pltpu.SemaphoreType.DMA((count,)),
        ],
        compiler_params=pltpu.CompilerParams(
            collective_id=0, has_side_effects=True, vmem_limit_bytes=40 * 1024 * 1024
        ),
    )(
        init_states.reshape(flat),
        forcing.reshape(flat),
        damp.reshape(flat),
        kappa_x[None],
        kappa_y[None],
        kappa_z[None],
        sea_tiles,
        phases,
    )
    return out.reshape(init_states.shape)


def choose(init_states, forcing, damp, kappa_x, kappa_y, kappa_z, sea_tiles, phases):
    count = lax.axis_size("tm") * lax.axis_size("space")
    n_t, slabs, nx, rows, nz = init_states.shape
    ny = lax.axis_size("space") * rows
    per = count // n_t
    fits = (
        slabs == 1
        and count % n_t == 0
        and nz == LANES
        and nx % LANES == 0
        and nz % per == 0
        and (nz // per * rows) % 8 == 0
        and (HALO * rows) % 8 == 0
        and nz // per + 2 * HALO <= nz
        and ny <= LANES
        and ny & (ny - 1) == 0
        and sea_tiles.shape[1] == 1
        and lax.axis_size("space") * (nz // per + 2 * HALO) * rows <= 512
    )
    run = whole_period if fits else body
    return run(init_states, forcing, damp, kappa_x, kappa_y, kappa_z, sea_tiles, phases)


def solution(mesh):
    return jax.shard_map(
        choose,
        mesh=mesh,
        in_specs=(
            P(None, "tm", None, "space", None),
            P(None, None, "space", None),
            P(None, None, "space", None),
            P(),
            P(),
            P(),
            P(),
            P("tm"),
        ),
        out_specs=P(None, "tm", None, "space", None),
        check_vma=False,
    )
```

```python
import functools
import math

import jax
import jax.numpy as jnp
from jax import lax
from jax.experimental import pallas as pl
from jax.experimental.pallas import tpu as pltpu
from jax.sharding import PartitionSpec as P

STEPS = 2
ITERS = 2
TILE = 16
PHASES = 12


def shifted(array, axis, by):
    devices = lax.axis_size(axis)
    return lax.ppermute(array, axis, [(i, (i + by) % devices) for i in range(devices)])


def line_inverse(kappa):
    face = 0.5 * (kappa[1:] + kappa[:-1])
    zero = jnp.zeros((1,), kappa.dtype)
    left = jnp.concatenate([zero, face])
    right = jnp.concatenate([face, zero])
    identity = jnp.eye(kappa.shape[0], dtype=kappa.dtype)
    return lax.linalg.tridiagonal_solve(-left, 1.0 + left + right, -right, identity)


def solve_lines(field, inverse):
    return jnp.matmul(inverse, field, precision=lax.Precision.HIGHEST)


def solve_x(field, inverse):
    shape = field.shape
    flat = field.reshape(shape[0], shape[1], shape[2], shape[3] * shape[4])
    return solve_lines(flat, inverse).reshape(shape)


def vertical_mix(field, kappa_z):
    face = 0.5 * (kappa_z[1:] + kappa_z[:-1])
    flux = face * (field[..., 1:] - field[..., :-1])
    zeros = jnp.zeros(field.shape[:-1] + (1,), field.dtype)
    flux = jnp.concatenate([zeros, flux, zeros], axis=-1)
    return field + flux[..., 1:] - flux[..., :-1]


def compose(earlier, later):
    return (earlier[0] * later[0], later[0] * earlier[1] + later[1])


def column_pass(field, inverse_y):
    return lax.all_to_all(
        solve_lines(
            lax.all_to_all(field, "space", split_axis=2, concat_axis=3, tiled=True), inverse_y
        ),
        "space",
        split_axis=3,
        concat_axis=2,
        tiled=True,
    )


def body(init_states, forcing, damp, kappa_x, kappa_y, kappa_z, sea_tiles, phases):
    row_count = init_states.shape[3]
    inverse_x = line_inverse(kappa_x)
    inverse_y = line_inverse(kappa_y)
    tiles = sea_tiles.astype(jnp.float32)
    sea = jnp.repeat(jnp.repeat(tiles, TILE, axis=0), TILE, axis=1)
    sea_rows = lax.dynamic_slice_in_dim(sea, lax.axis_index("space") * row_count, row_count, 1)
    source = (forcing * sea_rows[None, :, :, None])[:, None]
    phase_float = phases.astype(jnp.float32)
    weight = 1.0 + 0.5 * jnp.cos(2.0 * math.pi * phase_float / PHASES)
    factors = jnp.exp(weight[None, :, None, None, None] * jnp.log(damp)[:, None])
    states = init_states
    for iteration in range(ITERS):
        field = states
        for step in range(STEPS):
            amplitude = jnp.cos(2.0 * math.pi * (phase_float * STEPS + step) / (PHASES * STEPS))[
                None, :, None, None, None
            ]
            if step % 2 == 0:
                field = column_pass(solve_x(field, inverse_x), inverse_y)
            else:
                field = solve_x(column_pass(field, inverse_y), inverse_x)
            field = vertical_mix(field, kappa_z) + amplitude * source
        offsets = field - factors * states
        own_factor = factors[:, 0]
        own_offset = offsets[:, 0]
        own = (own_factor, own_offset)
        ident = (jnp.ones_like(own_factor), jnp.zeros_like(own_offset))
        count = lax.axis_size("tm")
        here = lax.axis_index("tm")
        lower_part = ident
        upper_part = ident
        moving = jnp.stack([own_factor, own_offset])
        for turn in range(1, count):
            moving = shifted(moving, "tm", 1)
            piece = (moving[0], moving[1])
            anchor = (here - turn) % count
            before = anchor < here
            joined_low = compose(piece, lower_part)
            joined_high = compose(piece, upper_part)
            lower_part = (
                jnp.where(before, joined_low[0], lower_part[0]),
                jnp.where(before, joined_low[1], lower_part[1]),
            )
            upper_part = (
                jnp.where(before, upper_part[0], joined_high[0]),
                jnp.where(before, upper_part[1], joined_high[1]),
            )
        period = compose(compose(lower_part, own), upper_part)
        first = period[1] / (1.0 - period[0])
        start = lower_part[0] * first + lower_part[1]
        fresh = [start]
        states = jnp.stack(fresh, axis=1)
    return states


LANES = 128
HALO = 2 * ITERS
MESH = pl.DeviceIdType.MESH


def dot(a, b):
    return jnp.dot(a, b, precision=lax.Precision.HIGHEST, preferred_element_type=jnp.float32)


def parts(a):
    high = a.astype(jnp.bfloat16)
    return high, (a - high.astype(jnp.float32)).astype(jnp.bfloat16)


def dot3(a, b):
    once = functools.partial(jnp.dot, preferred_element_type=jnp.float32)
    return once(a[0], b[0]) + (once(a[0], b[1]) + once(a[1], b[0]))


def iota(shape, axis):
    return lax.broadcasted_iota(jnp.int32, shape, axis)


def faces(kappa_row, n):
    row, col = iota((n, n), 0), iota((n, n), 1)
    own = jnp.sum(jnp.where(row == col, kappa_row, 0.0), axis=1, keepdims=True)
    face = 0.5 * (own + kappa_row)
    below = jnp.where(col == row - 1, face, 0.0)
    above = jnp.where(col == row + 1, face, 0.0)
    return (
        jnp.sum(below, axis=1, keepdims=True),
        jnp.sum(above, axis=1, keepdims=True),
        below + above,
    )


def reduced_inverse(kappa_row, n):
    lower, upper, _ = faces(kappa_row, n)
    shape = (n, LANES)
    a = jnp.broadcast_to(-lower, shape)
    c = jnp.broadcast_to(-upper, shape)
    b = 1.0 - a - c
    blocks = [
        (iota(shape, 0) == iota(shape, 1) + LANES * j).astype(jnp.float32)
        for j in range(max(n // LANES, 1))
    ]
    s = 1
    while s < n:
        before = functools.partial(pltpu.roll, shift=s, axis=0)
        after = functools.partial(pltpu.roll, shift=n - s, axis=0)
        alpha = -a / before(b)
        gamma = -c / after(b)
        blocks = [d + alpha * before(d) + gamma * after(d) for d in blocks]
        b = b + alpha * before(c) + gamma * after(a)
        a, c = alpha * before(a), gamma * after(c)
        s *= 2
    inverse = 1.0 / b
    return [d * inverse for d in blocks]


def period_kernel(
    size, u_hbm, f_hbm, damp_hbm, kx_hbm, ky_hbm, kz_hbm, sea_hbm, phase_ref, out_ref,
    u_ref, f_ref, damp_ref, kx_ref, ky_ref, kz_ref, sea_ref, fetched, inverse_p, split,
    ubuf, fbuf, pbuf, xbuf, dbuf, qbuf, obuf, rbuf, g_ref, a_ref, state, factor, source, offset_ref,
    u_send, u_recv, f_send, f_recv, p_send, p_recv, o_send, o_recv,
):
    n_tm, n_sp, n_t, nx, rows, nz = size
    count = n_tm * n_sp
    per = count // n_t
    chunk = nz // per
    window = chunk + 2 * HALO
    halves = nx // LANES
    wrows = window * rows
    crows = chunk * rows
    all_rows = n_sp * wrows
    ny = n_sp * rows

    here = lax.axis_index("tm")
    spot = lax.axis_index("space")
    me = here * n_sp + spot

    def window_start(k):
        return jnp.minimum(jnp.maximum(k * chunk - HALO, 0), nz - window)

    def window_rows(k):
        return pl.ds(pl.multiple_of(window_start(k) * rows, 8), wrows)

    def chunk_rows(k):
        return pl.ds(pl.multiple_of(k * crows, 8), crows)

    def device(index):
        return {"tm": index // n_sp, "space": index % n_sp}

    pairs = (
        (damp_hbm, damp_ref),
        (f_hbm, f_ref),
        (u_hbm, u_ref),
        (kx_hbm, kx_ref),
        (ky_hbm, ky_ref),
        (kz_hbm, kz_ref),
        (sea_hbm, sea_ref),
    )
    fetches = [
        pltpu.make_async_copy(far, near, fetched.at[i]) for i, (far, near) in enumerate(pairs)
    ]
    for fetch in fetches:
        fetch.start()

    barrier = pltpu.get_barrier_semaphore()

    @pl.loop(1, count)
    def greet(offset):
        pl.semaphore_signal(
            barrier, inc=1, device_id=device((me + offset) % count), device_id_type=MESH
        )

    def turn(ref, buf, where):
        for t in range(n_t):
            for half in range(halves):
                for y in range(rows):
                    part = ref[t, pl.ds(half * LANES * rows + y, LANES, stride=rows), :]
                    buf[(t, *where, half, pl.ds(y, nz, stride=rows), slice(None))] = part.T

    pbuf[...] = jnp.full((8, LANES), phase_ref[0].astype(jnp.float32))

    my_t, my_k = me // per, me % per
    my_start = window_start(my_k)

    own_copies = [
        pltpu.make_async_copy(
            ubuf.at[my_t, :, window_rows(my_k), :], xbuf.at[here, spot], u_recv.at[me]
        ),
        pltpu.make_async_copy(
            fbuf.at[my_t, :, :, window_rows(my_k), :], dbuf.at[spot], f_recv.at[spot]
        ),
        pltpu.make_async_copy(pbuf, qbuf.at[here], p_recv.at[here]),
    ]

    def send_u(offset):
        index = (me + offset) % count
        return pltpu.make_async_remote_copy(
            src_ref=ubuf.at[index // per, :, window_rows(index % per), :],
            dst_ref=xbuf.at[here, spot],
            send_sem=u_send.at[offset],
            recv_sem=u_recv.at[me],
            device_id=device(index),
            device_id_type=MESH,
        )

    def send_f(offset):
        index = here * n_sp + (spot + offset) % n_sp
        return pltpu.make_async_remote_copy(
            src_ref=fbuf.at[index // per, :, :, window_rows(index % per), :],
            dst_ref=dbuf.at[spot],
            send_sem=f_send.at[offset],
            recv_sem=f_recv.at[spot],
            device_id=device(index),
            device_id_type=MESH,
        )

    def send_p(offset):
        return pltpu.make_async_remote_copy(
            src_ref=pbuf,
            dst_ref=qbuf.at[here],
            send_sem=p_send.at[offset],
            recv_sem=p_recv.at[here],
            device_id={"tm": (here + offset) % n_tm, "space": spot},
            device_id_type=MESH,
        )

    def send_o(index):
        inner = pl.multiple_of((my_k * chunk - my_start) * rows, 8)
        return pltpu.make_async_remote_copy(
            src_ref=obuf.at[index // n_sp, index % n_sp, :, pl.ds(inner, crows), :],
            dst_ref=rbuf.at[my_t, :, chunk_rows(my_k), :],
            send_sem=o_send.at[index],
            recv_sem=o_recv.at[me],
            device_id=device(index),
            device_id_type=MESH,
        )

    fetches[0].wait()
    turn(damp_ref, fbuf, (0,))
    fetches[1].wait()
    turn(f_ref, fbuf, (1,))
    pl.semaphore_wait(barrier, count - 1)

    @pl.loop(1, n_tm)
    def start_p(offset):
        send_p(offset).start()

    @pl.loop(1, n_sp)
    def start_f(offset):
        send_f(offset).start()

    own_copies[1].start()
    own_copies[2].start()
    fetches[2].wait()
    turn(u_ref, ubuf, ())

    @pl.loop(1, count)
    def start_u(offset):
        send_u(offset).start()

    own_copies[0].start()
    for fetch in fetches[3:]:
        fetch.wait()

    for half, block in enumerate(reduced_inverse(kx_ref[...], nx)):
        a_ref[0, :, half * LANES : (half + 1) * LANES] = block
    a_ref[1] = dot(a_ref[0], a_ref[0])
    q, j = iota((all_rows, ny), 0), iota((all_rows, ny), 1)
    line = (q // wrows) * rows + q % rows
    pick_y = (line == j).astype(jnp.float32)
    q, j = iota((LANES, all_rows), 1), iota((LANES, all_rows), 0)
    line = (q // wrows) * rows + q % rows
    pick_y_back = (line == j).astype(jnp.float32)
    big_y = dot(dot(pick_y, reduced_inverse(ky_ref[...], ny)[0]), pick_y_back)
    _, _, beside = faces(kz_ref[...], nz)
    identity = (iota((nz, nz), 0) == iota((nz, nz), 1)).astype(jnp.float32)
    vertical = beside + identity * (1.0 - jnp.sum(beside, axis=1, keepdims=True))
    q, j = iota((all_rows, nz), 0), iota((all_rows, nz), 1)
    pick_z = (my_start + (q % wrows) // rows == j).astype(jnp.float32)
    q, j = iota((nz, all_rows), 1), iota((nz, all_rows), 0)
    pick_z_back = (my_start + (q % wrows) // rows == j).astype(jnp.float32)
    g_ref[0] = big_y * dot(dot(pick_z, vertical), pick_z_back)
    g_ref[1] = dot(g_ref[0], g_ref[0])
    tile = (iota((nx // TILE, nx), 1) // TILE == iota((nx // TILE, nx), 0)).astype(jnp.float32)
    tiles = nx // TILE
    flags = jnp.where(
        iota((tiles, tiles), 0) == iota((tiles, tiles), 1), sea_ref[...].astype(jnp.float32), 0.0
    )
    sea = jnp.sum(jnp.sum(flags, axis=1, keepdims=True) * tile, axis=0, keepdims=True)
    g_parts, a_parts = parts(g_ref[1]), parts(a_ref[1])
    for i in range(2):
        split[0, i, :all_rows, :all_rows] = g_parts[i]
        split[1, i, :nx, :nx] = a_parts[i]

    def gathered(ref, where):
        return jnp.concatenate(
            [ref[where(half)].reshape(all_rows, LANES) for half in range(halves)], axis=1
        )

    own_copies[1].wait()
    own_copies[2].wait()

    @pl.loop(1, n_tm)
    def wait_p(offset):
        index = (here + n_tm - offset) % n_tm
        pltpu.make_async_copy(qbuf.at[index], qbuf.at[index], p_recv.at[index]).wait()

    @pl.loop(1, n_sp)
    def wait_f(offset):
        index = (spot + n_sp - offset) % n_sp
        pltpu.make_async_copy(dbuf.at[index], dbuf.at[index], f_recv.at[index]).wait()

    source[1] = gathered(dbuf, lambda half: (slice(None), 1, half)) * sea
    source[0] = dot(dot(g_ref[0], source[1]), a_ref[0])

    @pl.loop(0, n_tm)
    def make_factors(n):
        log_damp = jnp.log(gathered(dbuf, lambda half: (slice(None), 0, half)))
        phase = qbuf[n]
        weight = 1.0 + 0.5 * jnp.cos(2.0 * math.pi * phase / PHASES)
        first = jnp.cos(2.0 * math.pi * (phase * STEPS) / (PHASES * STEPS))
        second = jnp.cos(2.0 * math.pi * (phase * STEPS + 1) / (PHASES * STEPS))

        def wide(values):
            return jnp.concatenate([values[:1]] * halves, axis=1)

        factor[n] = jnp.exp(wide(weight) * log_damp)
        offset_ref[n] = wide(first) * source[0] + wide(second) * source[1]

    product = factor[0]
    for n in range(1, n_tm):
        product = factor[n] * product
    inverse_p[...] = 1.0 / (1.0 - product)

    def fine(n, field):
        g_split = split[0, 0, :all_rows, :all_rows], split[0, 1, :all_rows, :all_rows]
        a_split = split[1, 0, :nx, :nx], split[1, 1, :nx, :nx]
        moved = dot3(parts(dot3(g_split, parts(field))), a_split)
        state[n] = moved + offset_ref[n] - factor[n] * field

    own_copies[0].wait()

    @pl.loop(1, n_tm + 1)
    def fine_first(turned):
        n = (here + n_tm - turned) % n_tm

        @pl.loop(0, n_sp)
        def wait_u(r):
            @pl.when(n * n_sp + r != me)
            def _():
                slot = xbuf.at[n, r]
                pltpu.make_async_copy(slot, slot, u_recv.at[n * n_sp + r]).wait()

        fine(n, gathered(xbuf, lambda half: (n, slice(None), half)))

    def solve(r, keep):
        block = pl.ds(pl.multiple_of(r * wrows, 8), wrows)
        factors = [factor[n, block, :] for n in range(n_tm)]
        offsets = [state[n, block, :] for n in range(n_tm)]
        total = offsets[0]
        for n in range(1, n_tm):
            total = factors[n] * total + offsets[n]
        fresh = total * inverse_p[block, :]
        for n in range(n_tm):
            keep(n, block, fresh)
            fresh = factors[n] * fresh + offsets[n]

    def keep_state(n, block, values):
        state[n, block, :] = values

    for iteration in range(1, ITERS):
        pl.loop(0, n_sp)(lambda r: solve(r, keep_state))
        pl.loop(0, n_tm)(lambda n: fine(n, state[n]))

    inner = pl.multiple_of((my_k * chunk - my_start) * rows, 8)
    back = pltpu.make_async_copy(
        obuf.at[here, spot, :, pl.ds(inner, crows), :],
        rbuf.at[my_t, :, chunk_rows(my_k), :],
        o_recv.at[me],
    )

    @pl.loop(1, n_sp + 1)
    def solve_last(turned):
        r = (spot + turned) % n_sp

        def keep_out(n, block, values):
            for half in range(halves):
                obuf[n, r, half] = values[:, half * LANES : (half + 1) * LANES]

        solve(r, keep_out)
        for n in range(n_tm):

            @pl.when(n * n_sp + r != me)
            def _():
                send_o(n * n_sp + r).start()

    back.start()
    back.wait()

    for t in range(n_t):

        @pl.loop(t * per, (t + 1) * per)
        def wait_o(index):
            @pl.when(index != me)
            def _():
                slot = rbuf.at[t, :, chunk_rows(index % per), :]
                pltpu.make_async_copy(slot, slot, o_recv.at[index]).wait()

        for half in range(halves):
            for y in range(rows):
                part = rbuf[t, half, pl.ds(y, nz, stride=rows), :]
                out_ref[t, pl.ds(half * LANES * rows + y, LANES, stride=rows), :] = part.T

    @pl.loop(1, count)
    def sent(offset):
        send_u(offset).wait_send()
        send_o((me + offset) % count).wait_send()

    @pl.loop(1, n_sp)
    def sent_f(offset):
        send_f(offset).wait_send()

    @pl.loop(1, n_tm)
    def sent_p(offset):
        send_p(offset).wait_send()


def whole_period(init_states, forcing, damp, kappa_x, kappa_y, kappa_z, sea_tiles, phases):
    n_tm, n_sp = lax.axis_size("tm"), lax.axis_size("space")
    n_t, _, nx, rows, nz = init_states.shape
    count = n_tm * n_sp
    chunk = nz // (count // n_t)
    window = chunk + 2 * HALO
    halves = nx // LANES
    wrows = window * rows
    all_rows = n_sp * wrows
    flat = (n_t, nx * rows, nz)
    vmem = pl.BlockSpec(memory_space=pltpu.VMEM)
    f32 = jnp.float32
    out = pl.pallas_call(
        functools.partial(period_kernel, (n_tm, n_sp, n_t, nx, rows, nz)),
        out_shape=jax.ShapeDtypeStruct(flat, f32),
        in_specs=[pl.BlockSpec(memory_space=pltpu.HBM)] * 7 + [pl.BlockSpec(memory_space=pltpu.SMEM)],
        out_specs=vmem,
        scratch_shapes=[
            pltpu.VMEM(flat, f32),
            pltpu.VMEM(flat, f32),
            pltpu.VMEM(flat, f32),
            pltpu.VMEM((1, nx), f32),
            pltpu.VMEM((1, kappa_y.shape[0]), f32),
            pltpu.VMEM((1, nz), f32),
            pltpu.VMEM((1, sea_tiles.shape[0]), jnp.int32),
            pltpu.SemaphoreType.DMA((7,)),
            pltpu.VMEM((all_rows, nx), f32),
            pltpu.VMEM((2, 2, max(all_rows, nx), max(all_rows, nx)), jnp.bfloat16),
            pltpu.VMEM((n_t, halves, nz * rows, LANES), f32),
            pltpu.VMEM((n_t, 2, halves, nz * rows, LANES), f32),
            pltpu.VMEM((8, LANES), f32),
            pltpu.VMEM((n_tm, n_sp, halves, wrows, LANES), f32),
            pltpu.VMEM((n_sp, 2, halves, wrows, LANES), f32),
            pltpu.VMEM((n_tm, 8, LANES), f32),
            pltpu.VMEM((n_tm, n_sp, halves, wrows, LANES), f32),
            pltpu.VMEM((n_t, halves, nz * rows, LANES), f32),
            pltpu.VMEM((2, all_rows, all_rows), f32),
            pltpu.VMEM((2, nx, nx), f32),
            pltpu.VMEM((n_tm, all_rows, nx), f32),
            pltpu.VMEM((n_tm, all_rows, nx), f32),
            pltpu.VMEM((2, all_rows, nx), f32),
            pltpu.VMEM((n_tm, all_rows, nx), f32),
            pltpu.SemaphoreType.DMA((count,)),
            pltpu.SemaphoreType.DMA((count,)),
            pltpu.SemaphoreType.DMA((n_sp,)),
            pltpu.SemaphoreType.DMA((n_sp,)),
            pltpu.SemaphoreType.DMA((n_tm,)),
            pltpu.SemaphoreType.DMA((n_tm,)),
            pltpu.SemaphoreType.DMA((count,)),
            pltpu.SemaphoreType.DMA((count,)),
        ],
        compiler_params=pltpu.CompilerParams(
            collective_id=0, has_side_effects=True, vmem_limit_bytes=63 * 1024 * 1024
        ),
    )(
        init_states.reshape(flat),
        forcing.reshape(flat),
        damp.reshape(flat),
        kappa_x[None],
        kappa_y[None],
        kappa_z[None],
        sea_tiles.reshape(1, -1),
        phases,
    )
    return out.reshape(init_states.shape)


def choose(init_states, forcing, damp, kappa_x, kappa_y, kappa_z, sea_tiles, phases):
    count = lax.axis_size("tm") * lax.axis_size("space")
    n_t, slabs, nx, rows, nz = init_states.shape
    ny = lax.axis_size("space") * rows
    per = count // n_t
    fits = (
        slabs == 1
        and count % n_t == 0
        and nz == LANES
        and nx % LANES == 0
        and nz % per == 0
        and (nz // per * rows) % 8 == 0
        and (HALO * rows) % 8 == 0
        and nz // per + 2 * HALO <= nz
        and ny <= LANES
        and ny & (ny - 1) == 0
        and sea_tiles.shape[1] == 1
        and lax.axis_size("space") * (nz // per + 2 * HALO) * rows <= 512
    )
    run = whole_period if fits else body
    return run(init_states, forcing, damp, kappa_x, kappa_y, kappa_z, sea_tiles, phases)


def solution(mesh):
    return jax.shard_map(
        choose,
        mesh=mesh,
        in_specs=(
            P(None, "tm", None, "space", None),
            P(None, None, "space", None),
            P(None, None, "space", None),
            P(),
            P(),
            P(),
            P(),
            P("tm"),
        ),
        out_specs=P(None, "tm", None, "space", None),
        check_vma=False,
    )
```

```python
import functools
import math

import jax
import jax.numpy as jnp
from jax import lax
from jax.experimental import pallas as pl
from jax.experimental.pallas import tpu as pltpu
from jax.sharding import PartitionSpec as P

STEPS = 2
ITERS = 2
TILE = 16
PHASES = 12


def shifted(array, axis, by):
    devices = lax.axis_size(axis)
    return lax.ppermute(array, axis, [(i, (i + by) % devices) for i in range(devices)])


def line_inverse(kappa):
    face = 0.5 * (kappa[1:] + kappa[:-1])
    zero = jnp.zeros((1,), kappa.dtype)
    left = jnp.concatenate([zero, face])
    right = jnp.concatenate([face, zero])
    identity = jnp.eye(kappa.shape[0], dtype=kappa.dtype)
    return lax.linalg.tridiagonal_solve(-left, 1.0 + left + right, -right, identity)


def solve_lines(field, inverse):
    return jnp.matmul(inverse, field, precision=lax.Precision.HIGHEST)


def solve_x(field, inverse):
    shape = field.shape
    flat = field.reshape(shape[0], shape[1], shape[2], shape[3] * shape[4])
    return solve_lines(flat, inverse).reshape(shape)


def vertical_mix(field, kappa_z):
    face = 0.5 * (kappa_z[1:] + kappa_z[:-1])
    flux = face * (field[..., 1:] - field[..., :-1])
    zeros = jnp.zeros(field.shape[:-1] + (1,), field.dtype)
    flux = jnp.concatenate([zeros, flux, zeros], axis=-1)
    return field + flux[..., 1:] - flux[..., :-1]


def compose(earlier, later):
    return (earlier[0] * later[0], later[0] * earlier[1] + later[1])


def column_pass(field, inverse_y):
    return lax.all_to_all(
        solve_lines(
            lax.all_to_all(field, "space", split_axis=2, concat_axis=3, tiled=True), inverse_y
        ),
        "space",
        split_axis=3,
        concat_axis=2,
        tiled=True,
    )


def body(init_states, forcing, damp, kappa_x, kappa_y, kappa_z, sea_tiles, phases):
    row_count = init_states.shape[3]
    inverse_x = line_inverse(kappa_x)
    inverse_y = line_inverse(kappa_y)
    tiles = sea_tiles.astype(jnp.float32)
    sea = jnp.repeat(jnp.repeat(tiles, TILE, axis=0), TILE, axis=1)
    sea_rows = lax.dynamic_slice_in_dim(sea, lax.axis_index("space") * row_count, row_count, 1)
    source = (forcing * sea_rows[None, :, :, None])[:, None]
    phase_float = phases.astype(jnp.float32)
    weight = 1.0 + 0.5 * jnp.cos(2.0 * math.pi * phase_float / PHASES)
    factors = jnp.exp(weight[None, :, None, None, None] * jnp.log(damp)[:, None])
    states = init_states
    for iteration in range(ITERS):
        field = states
        for step in range(STEPS):
            amplitude = jnp.cos(2.0 * math.pi * (phase_float * STEPS + step) / (PHASES * STEPS))[
                None, :, None, None, None
            ]
            if step % 2 == 0:
                field = column_pass(solve_x(field, inverse_x), inverse_y)
            else:
                field = solve_x(column_pass(field, inverse_y), inverse_x)
            field = vertical_mix(field, kappa_z) + amplitude * source
        offsets = field - factors * states
        own_factor = factors[:, 0]
        own_offset = offsets[:, 0]
        own = (own_factor, own_offset)
        ident = (jnp.ones_like(own_factor), jnp.zeros_like(own_offset))
        count = lax.axis_size("tm")
        here = lax.axis_index("tm")
        lower_part = ident
        upper_part = ident
        moving = jnp.stack([own_factor, own_offset])
        for turn in range(1, count):
            moving = shifted(moving, "tm", 1)
            piece = (moving[0], moving[1])
            anchor = (here - turn) % count
            before = anchor < here
            joined_low = compose(piece, lower_part)
            joined_high = compose(piece, upper_part)
            lower_part = (
                jnp.where(before, joined_low[0], lower_part[0]),
                jnp.where(before, joined_low[1], lower_part[1]),
            )
            upper_part = (
                jnp.where(before, upper_part[0], joined_high[0]),
                jnp.where(before, upper_part[1], joined_high[1]),
            )
        period = compose(compose(lower_part, own), upper_part)
        first = period[1] / (1.0 - period[0])
        start = lower_part[0] * first + lower_part[1]
        fresh = [start]
        states = jnp.stack(fresh, axis=1)
    return states


LANES = 128
HALO = 2 * ITERS
MESH = pl.DeviceIdType.MESH


def dot(a, b):
    return jnp.dot(a, b, precision=lax.Precision.HIGHEST, preferred_element_type=jnp.float32)


def parts(a):
    high = a.astype(jnp.bfloat16)
    return high, (a - high.astype(jnp.float32)).astype(jnp.bfloat16)


def dot3(a, b):
    once = functools.partial(jnp.dot, preferred_element_type=jnp.float32)
    return once(a[0], b[0]) + (once(a[0], b[1]) + once(a[1], b[0]))


def iota(shape, axis):
    return lax.broadcasted_iota(jnp.int32, shape, axis)


def faces(kappa_row, n):
    row, col = iota((n, n), 0), iota((n, n), 1)
    own = jnp.sum(jnp.where(row == col, kappa_row, 0.0), axis=1, keepdims=True)
    face = 0.5 * (own + kappa_row)
    below = jnp.where(col == row - 1, face, 0.0)
    above = jnp.where(col == row + 1, face, 0.0)
    return (
        jnp.sum(below, axis=1, keepdims=True),
        jnp.sum(above, axis=1, keepdims=True),
        below + above,
    )


def reduced_inverse(kappa_row, n):
    lower, upper, _ = faces(kappa_row, n)
    shape = (n, LANES)
    a = jnp.broadcast_to(-lower, shape)
    c = jnp.broadcast_to(-upper, shape)
    b = 1.0 - a - c
    blocks = [
        (iota(shape, 0) == iota(shape, 1) + LANES * j).astype(jnp.float32)
        for j in range(max(n // LANES, 1))
    ]
    s = 1
    while s < n:
        before = functools.partial(pltpu.roll, shift=s, axis=0)
        after = functools.partial(pltpu.roll, shift=n - s, axis=0)
        alpha = -a / before(b)
        gamma = -c / after(b)
        blocks = [d + alpha * before(d) + gamma * after(d) for d in blocks]
        b = b + alpha * before(c) + gamma * after(a)
        a, c = alpha * before(a), gamma * after(c)
        s *= 2
    inverse = 1.0 / b
    return [d * inverse for d in blocks]


def period_kernel(
    size, u_hbm, f_hbm, damp_hbm, kx_hbm, ky_hbm, kz_hbm, sea_hbm, phase_ref, out_ref,
    u_ref, f_ref, damp_ref, kx_ref, ky_ref, kz_ref, sea_ref, fetched, inverse_p, split, ends,
    ubuf, fbuf, pbuf, xbuf, dbuf, qbuf, obuf, rbuf, g_ref, a_ref, state, factor, source, offset_ref,
    u_send, u_recv, f_send, f_recv, p_send, p_recv, o_send, o_recv,
):
    n_tm, n_sp, n_t, nx, rows, nz = size
    count = n_tm * n_sp
    per = count // n_t
    chunk = nz // per
    window = chunk + 2 * HALO
    halves = nx // LANES
    wrows = window * rows
    crows = chunk * rows
    all_rows = n_sp * wrows
    ny = n_sp * rows

    here = lax.axis_index("tm")
    spot = lax.axis_index("space")
    me = here * n_sp + spot

    def window_start(k):
        return jnp.minimum(jnp.maximum(k * chunk - HALO, 0), nz - window)

    def window_rows(k):
        return pl.ds(pl.multiple_of(window_start(k) * rows, 8), wrows)

    def chunk_rows(k):
        return pl.ds(pl.multiple_of(k * crows, 8), crows)

    def device(index):
        return {"tm": index // n_sp, "space": index % n_sp}

    pairs = (
        (damp_hbm, damp_ref),
        (f_hbm, f_ref),
        (u_hbm, u_ref),
        (kx_hbm, kx_ref),
        (ky_hbm, ky_ref),
        (kz_hbm, kz_ref),
        (sea_hbm, sea_ref),
    )
    fetches = [
        pltpu.make_async_copy(far, near, fetched.at[i]) for i, (far, near) in enumerate(pairs)
    ]
    for fetch in fetches:
        fetch.start()

    barrier = pltpu.get_barrier_semaphore()

    @pl.loop(1, count)
    def greet(offset):
        pl.semaphore_signal(
            barrier, inc=1, device_id=device((me + offset) % count), device_id_type=MESH
        )

    def turn(ref, buf, where):
        for t in range(n_t):
            for half in range(halves):
                for y in range(rows):
                    part = ref[t, pl.ds(half * LANES * rows + y, LANES, stride=rows), :]
                    buf[(t, *where, half, pl.ds(y, nz, stride=rows), slice(None))] = part.T

    pbuf[...] = jnp.full((8, LANES), phase_ref[0].astype(jnp.float32))

    my_t, my_k = me // per, me % per
    my_start = window_start(my_k)

    own_copies = [
        pltpu.make_async_copy(
            ubuf.at[my_t, :, window_rows(my_k), :], xbuf.at[here, spot], u_recv.at[me]
        ),
        pltpu.make_async_copy(
            fbuf.at[my_t, :, :, window_rows(my_k), :], dbuf.at[spot], f_recv.at[spot]
        ),
        pltpu.make_async_copy(pbuf, qbuf.at[here], p_recv.at[here]),
    ]

    def send_u(offset):
        index = (me + offset) % count
        return pltpu.make_async_remote_copy(
            src_ref=ubuf.at[index // per, :, window_rows(index % per), :],
            dst_ref=xbuf.at[here, spot],
            send_sem=u_send.at[offset],
            recv_sem=u_recv.at[me],
            device_id=device(index),
            device_id_type=MESH,
        )

    def send_f(offset):
        index = here * n_sp + (spot + offset) % n_sp
        return pltpu.make_async_remote_copy(
            src_ref=fbuf.at[index // per, :, :, window_rows(index % per), :],
            dst_ref=dbuf.at[spot],
            send_sem=f_send.at[offset],
            recv_sem=f_recv.at[spot],
            device_id=device(index),
            device_id_type=MESH,
        )

    def send_p(offset):
        return pltpu.make_async_remote_copy(
            src_ref=pbuf,
            dst_ref=qbuf.at[here],
            send_sem=p_send.at[offset],
            recv_sem=p_recv.at[here],
            device_id={"tm": (here + offset) % n_tm, "space": spot},
            device_id_type=MESH,
        )

    def send_o(index):
        inner = pl.multiple_of((my_k * chunk - my_start) * rows, 8)
        return pltpu.make_async_remote_copy(
            src_ref=obuf.at[index // n_sp, index % n_sp, :, pl.ds(inner, crows), :],
            dst_ref=rbuf.at[my_t, :, chunk_rows(my_k), :],
            send_sem=o_send.at[index],
            recv_sem=o_recv.at[me],
            device_id=device(index),
            device_id_type=MESH,
        )

    fetches[0].wait()
    turn(damp_ref, fbuf, (0,))
    fetches[1].wait()
    turn(f_ref, fbuf, (1,))
    pl.semaphore_wait(barrier, count - 1)

    @pl.loop(1, n_tm)
    def start_p(offset):
        send_p(offset).start()

    @pl.loop(1, n_sp)
    def start_f(offset):
        send_f(offset).start()

    own_copies[1].start()
    own_copies[2].start()
    fetches[2].wait()
    turn(u_ref, ubuf, ())

    @pl.loop(1, count)
    def start_u(offset):
        send_u(offset).start()

    own_copies[0].start()
    for fetch in fetches[3:]:
        fetch.wait()

    for half, block in enumerate(reduced_inverse(kx_ref[...], nx)):
        a_ref[0, :, half * LANES : (half + 1) * LANES] = block
    a_ref[1] = dot(a_ref[0], a_ref[0])
    q, j = iota((all_rows, ny), 0), iota((all_rows, ny), 1)
    line = (q // wrows) * rows + q % rows
    pick_y = (line == j).astype(jnp.float32)
    q, j = iota((LANES, all_rows), 1), iota((LANES, all_rows), 0)
    line = (q // wrows) * rows + q % rows
    pick_y_back = (line == j).astype(jnp.float32)
    big_y = dot(dot(pick_y, reduced_inverse(ky_ref[...], ny)[0]), pick_y_back)
    _, _, beside = faces(kz_ref[...], nz)
    identity = (iota((nz, nz), 0) == iota((nz, nz), 1)).astype(jnp.float32)
    vertical = beside + identity * (1.0 - jnp.sum(beside, axis=1, keepdims=True))
    q, j = iota((all_rows, nz), 0), iota((all_rows, nz), 1)
    pick_z = (my_start + (q % wrows) // rows == j).astype(jnp.float32)
    q, j = iota((nz, all_rows), 1), iota((nz, all_rows), 0)
    pick_z_back = (my_start + (q % wrows) // rows == j).astype(jnp.float32)
    g_ref[0] = big_y * dot(dot(pick_z, vertical), pick_z_back)
    g_ref[1] = dot(g_ref[0], g_ref[0])
    tile = (iota((nx // TILE, nx), 1) // TILE == iota((nx // TILE, nx), 0)).astype(jnp.float32)
    tiles = nx // TILE
    flags = jnp.where(
        iota((tiles, tiles), 0) == iota((tiles, tiles), 1), sea_ref[...].astype(jnp.float32), 0.0
    )
    sea = jnp.sum(jnp.sum(flags, axis=1, keepdims=True) * tile, axis=0, keepdims=True)
    g_parts, a_parts = parts(g_ref[1]), parts(a_ref[1])
    for i in range(2):
        split[0, i, :all_rows, :all_rows] = g_parts[i]
        split[1, i, :nx, :nx] = a_parts[i]

    def gathered(ref, where):
        return jnp.concatenate(
            [ref[where(half)].reshape(all_rows, LANES) for half in range(halves)], axis=1
        )

    own_copies[1].wait()
    own_copies[2].wait()

    @pl.loop(1, n_tm)
    def wait_p(offset):
        index = (here + n_tm - offset) % n_tm
        pltpu.make_async_copy(qbuf.at[index], qbuf.at[index], p_recv.at[index]).wait()

    @pl.loop(1, n_sp)
    def wait_f(offset):
        index = (spot + n_sp - offset) % n_sp
        pltpu.make_async_copy(dbuf.at[index], dbuf.at[index], f_recv.at[index]).wait()

    source[1] = gathered(dbuf, lambda half: (slice(None), 1, half)) * sea
    source[0] = dot(dot(g_ref[0], source[1]), a_ref[0])

    @pl.loop(0, n_tm)
    def make_factors(n):
        log_damp = jnp.log(gathered(dbuf, lambda half: (slice(None), 0, half)))
        phase = qbuf[n]
        weight = 1.0 + 0.5 * jnp.cos(2.0 * math.pi * phase / PHASES)
        first = jnp.cos(2.0 * math.pi * (phase * STEPS) / (PHASES * STEPS))
        second = jnp.cos(2.0 * math.pi * (phase * STEPS + 1) / (PHASES * STEPS))

        def wide(values):
            return jnp.concatenate([values[:1]] * halves, axis=1)

        factor[n] = jnp.exp(wide(weight) * log_damp)
        offset_ref[n] = wide(first) * source[0] + wide(second) * source[1]

    product = factor[0]
    for n in range(1, n_tm):
        product = factor[n] * product
    inverse_p[...] = 1.0 / (1.0 - product)

    def fine(n, field):
        g_split = split[0, 0, :all_rows, :all_rows], split[0, 1, :all_rows, :all_rows]
        a_split = split[1, 0, :nx, :nx], split[1, 1, :nx, :nx]
        moved = dot3(parts(dot3(g_split, parts(field))), a_split)
        state[n] = moved + offset_ref[n] - factor[n] * field

    own_copies[0].wait()

    @pl.loop(1, n_tm + 1)
    def fine_first(turned):
        n = (here + n_tm - turned) % n_tm

        @pl.loop(0, n_sp)
        def wait_u(r):
            @pl.when(n * n_sp + r != me)
            def _():
                slot = xbuf.at[n, r]
                pltpu.make_async_copy(slot, slot, u_recv.at[n * n_sp + r]).wait()

        fine(n, gathered(xbuf, lambda half: (n, slice(None), half)))

    def fine_rows(n, block):
        field = state[n]
        g_split = split[0, 0, block, :all_rows], split[0, 1, block, :all_rows]
        a_split = split[1, 0, :nx, :nx], split[1, 1, :nx, :nx]
        moved = dot3(parts(dot3(g_split, parts(field))), a_split)
        ends[n, block, :] = moved + offset_ref[n, block, :] - factor[n, block, :] * state[n, block, :]

    def solve(r, held, keep):
        block = pl.ds(pl.multiple_of(r * wrows, 8), wrows)
        factors = [factor[n, block, :] for n in range(n_tm)]
        offsets = [held[n, block, :] for n in range(n_tm)]
        total = offsets[0]
        for n in range(1, n_tm):
            total = factors[n] * total + offsets[n]
        fresh = total * inverse_p[block, :]
        for n in range(n_tm):
            keep(n, block, fresh)
            fresh = factors[n] * fresh + offsets[n]

    def keep_state(n, block, values):
        state[n, block, :] = values

    for iteration in range(1, ITERS):
        pl.loop(0, n_sp)(lambda r: solve(r, state, keep_state))
        if iteration < ITERS - 1:
            pl.loop(0, n_tm)(lambda n: fine(n, state[n]))

    inner = pl.multiple_of((my_k * chunk - my_start) * rows, 8)
    back = pltpu.make_async_copy(
        obuf.at[here, spot, :, pl.ds(inner, crows), :],
        rbuf.at[my_t, :, chunk_rows(my_k), :],
        o_recv.at[me],
    )

    near_half = spot // (n_sp // 2)

    @pl.loop(1, 3)
    def last_half(turned_half):
        part = (near_half + turned_half) % 2
        block = pl.ds(pl.multiple_of(part * (all_rows // 2), 16), all_rows // 2)
        for n in range(n_tm):
            fine_rows(n, block)

        @pl.loop(1, n_sp // 2 + 1)
        def solve_last(turned):
            r = part * (n_sp // 2) + (spot + turned) % (n_sp // 2)

            def keep_out(n, rows_block, values):
                for half in range(halves):
                    obuf[n, r, half] = values[:, half * LANES : (half + 1) * LANES]

            solve(r, ends, keep_out)
            for n in range(n_tm):

                @pl.when(n * n_sp + r != me)
                def _():
                    send_o(n * n_sp + r).start()

    back.start()
    back.wait()

    for t in range(n_t):

        @pl.loop(t * per, (t + 1) * per)
        def wait_o(index):
            @pl.when(index != me)
            def _():
                slot = rbuf.at[t, :, chunk_rows(index % per), :]
                pltpu.make_async_copy(slot, slot, o_recv.at[index]).wait()

        for half in range(halves):
            for y in range(rows):
                part = rbuf[t, half, pl.ds(y, nz, stride=rows), :]
                out_ref[t, pl.ds(half * LANES * rows + y, LANES, stride=rows), :] = part.T

    @pl.loop(1, count)
    def sent(offset):
        send_u(offset).wait_send()
        send_o((me + offset) % count).wait_send()

    @pl.loop(1, n_sp)
    def sent_f(offset):
        send_f(offset).wait_send()

    @pl.loop(1, n_tm)
    def sent_p(offset):
        send_p(offset).wait_send()


def whole_period(init_states, forcing, damp, kappa_x, kappa_y, kappa_z, sea_tiles, phases):
    n_tm, n_sp = lax.axis_size("tm"), lax.axis_size("space")
    n_t, _, nx, rows, nz = init_states.shape
    count = n_tm * n_sp
    chunk = nz // (count // n_t)
    window = chunk + 2 * HALO
    halves = nx // LANES
    wrows = window * rows
    all_rows = n_sp * wrows
    flat = (n_t, nx * rows, nz)
    vmem = pl.BlockSpec(memory_space=pltpu.VMEM)
    f32 = jnp.float32
    out = pl.pallas_call(
        functools.partial(period_kernel, (n_tm, n_sp, n_t, nx, rows, nz)),
        out_shape=jax.ShapeDtypeStruct(flat, f32),
        in_specs=[pl.BlockSpec(memory_space=pltpu.HBM)] * 7 + [pl.BlockSpec(memory_space=pltpu.SMEM)],
        out_specs=vmem,
        scratch_shapes=[
            pltpu.VMEM(flat, f32),
            pltpu.VMEM(flat, f32),
            pltpu.VMEM(flat, f32),
            pltpu.VMEM((1, nx), f32),
            pltpu.VMEM((1, kappa_y.shape[0]), f32),
            pltpu.VMEM((1, nz), f32),
            pltpu.VMEM((1, sea_tiles.shape[0]), jnp.int32),
            pltpu.SemaphoreType.DMA((7,)),
            pltpu.VMEM((all_rows, nx), f32),
            pltpu.VMEM((2, 2, max(all_rows, nx), max(all_rows, nx)), jnp.bfloat16),
            pltpu.VMEM((n_tm, all_rows, nx), f32),
            pltpu.VMEM((n_t, halves, nz * rows, LANES), f32),
            pltpu.VMEM((n_t, 2, halves, nz * rows, LANES), f32),
            pltpu.VMEM((8, LANES), f32),
            pltpu.VMEM((n_tm, n_sp, halves, wrows, LANES), f32),
            pltpu.VMEM((n_sp, 2, halves, wrows, LANES), f32),
            pltpu.VMEM((n_tm, 8, LANES), f32),
            pltpu.VMEM((n_tm, n_sp, halves, wrows, LANES), f32),
            pltpu.VMEM((n_t, halves, nz * rows, LANES), f32),
            pltpu.VMEM((2, all_rows, all_rows), f32),
            pltpu.VMEM((2, nx, nx), f32),
            pltpu.VMEM((n_tm, all_rows, nx), f32),
            pltpu.VMEM((n_tm, all_rows, nx), f32),
            pltpu.VMEM((2, all_rows, nx), f32),
            pltpu.VMEM((n_tm, all_rows, nx), f32),
            pltpu.SemaphoreType.DMA((count,)),
            pltpu.SemaphoreType.DMA((count,)),
            pltpu.SemaphoreType.DMA((n_sp,)),
            pltpu.SemaphoreType.DMA((n_sp,)),
            pltpu.SemaphoreType.DMA((n_tm,)),
            pltpu.SemaphoreType.DMA((n_tm,)),
            pltpu.SemaphoreType.DMA((count,)),
            pltpu.SemaphoreType.DMA((count,)),
        ],
        compiler_params=pltpu.CompilerParams(
            collective_id=0, has_side_effects=True, vmem_limit_bytes=63 * 1024 * 1024
        ),
    )(
        init_states.reshape(flat),
        forcing.reshape(flat),
        damp.reshape(flat),
        kappa_x[None],
        kappa_y[None],
        kappa_z[None],
        sea_tiles.reshape(1, -1),
        phases,
    )
    return out.reshape(init_states.shape)


def choose(init_states, forcing, damp, kappa_x, kappa_y, kappa_z, sea_tiles, phases):
    count = lax.axis_size("tm") * lax.axis_size("space")
    n_t, slabs, nx, rows, nz = init_states.shape
    ny = lax.axis_size("space") * rows
    per = count // n_t
    fits = (
        slabs == 1
        and count % n_t == 0
        and nz == LANES
        and nx % LANES == 0
        and nz % per == 0
        and (nz // per * rows) % 8 == 0
        and (HALO * rows) % 8 == 0
        and nz // per + 2 * HALO <= nz
        and ny <= LANES
        and ny & (ny - 1) == 0
        and sea_tiles.shape[1] == 1
        and lax.axis_size("space") % 2 == 0
        and lax.axis_size("space") * (nz // per + 2 * HALO) * rows <= 512
    )
    run = whole_period if fits else body
    return run(init_states, forcing, damp, kappa_x, kappa_y, kappa_z, sea_tiles, phases)


def solution(mesh):
    return jax.shard_map(
        choose,
        mesh=mesh,
        in_specs=(
            P(None, "tm", None, "space", None),
            P(None, None, "space", None),
            P(None, None, "space", None),
            P(),
            P(),
            P(),
            P(),
            P("tm"),
        ),
        out_specs=P(None, "tm", None, "space", None),
        check_vma=False,
    )
```
